256 devices in a mesh: tm: 128 (over y_hi, x, z, core), chan: 2 (over y_lo).
Axes of the slice: x: 4, y: 4 (y_hi: 2, y_lo: 2; y = y_hi * 2 + y_lo), z: 8, core: 2. Of those that a mesh axis runs over, the one named last changes fastest.
Arguments:
- series: float32 [64, 65536], P('chan', 'tm'), may hold values from -200 to 200
- tail: float32 [64, 127], P('chan'), may hold values from -200 to 200
- excl: int32 [1], replicated, may hold values from 32 to 128
Outputs:
- profile: float32 [65536], P('tm')
The draws below stay inside these ranges and needn't reach their ends.
All inputs are finite; a program needn't handle non-finite values.
Results may differ from the reference program's by a relative error of at most 0.0003.
Values may be sent and summed in bfloat16 or wider, within the bound.
A program may use at most 128 MiB of HBM per device.

```python
import math
import jax
import jax.numpy as jnp
from jax import lax

C = 64
M = 128
S_DEV = 512
NT = 65536
N_TM = 128


def common_series(key):
    base = jax.random.fold_in(key, 4242)
    total = NT + M - 1
    factors = 4
    keys = jax.random.split(base, 6)
    rates = jnp.exp(jax.random.uniform(keys[0], (factors,), jnp.float32, jnp.log(0.005), jnp.log(0.1)))
    keepers = 1.0 - rates
    innovation = jax.random.normal(keys[1], (total, factors), jnp.float32)
    drive = jnp.sqrt(1.0 - keepers * keepers)

    def advance(state, entry):
        fresh = keepers * state + drive * entry
        return (fresh, fresh)
    unused, common = lax.scan(advance, jnp.zeros((factors,), jnp.float32), innovation)
    loadings = jax.random.normal(keys[2], (C, factors), jnp.float32)
    noise_level = jax.random.uniform(keys[3], (C, 1), jnp.float32, 0.3, 1.0)
    scales = jnp.exp(jax.random.uniform(keys[4], (C, 1), jnp.float32, 0.0, jnp.log(10.0)))
    noise = jax.random.normal(keys[5], (C, total), jnp.float32)
    values = scales * (jnp.dot(loadings, common.T) + noise_level * noise)
    return jnp.clip(values, -200.0, 200.0)


def draw_series(key, part):
    return common_series(key)[:, :NT]


def draw_tail(key, part):
    return common_series(key)[:, NT:]


def setup_inputs(seed: int = 0) -> dict:
    key_list = jax.random.split(jax.random.key(seed), 4)
    return {
        "series": draw_series(jax.random.fold_in(key_list[3], 71), 0),
        "tail": draw_tail(jax.random.fold_in(key_list[3], 71), 0),
        "excl": jax.random.randint(key_list[2], (1,), M // 4, M + 1).astype(jnp.int32),
    }


EPSILON = 1e-05
CEILING = 4.0

def normalize(extended, count, length, channels):
    starts = jnp.arange(length, dtype=jnp.int32)[:, None] + jnp.arange(count, dtype=jnp.int32)[None, :]
    windows = extended[:, starts]
    center = lax.optimization_barrier(jnp.mean(windows, axis=1, keepdims=True))
    shifted = windows - center
    spread = lax.optimization_barrier(jnp.mean(shifted * shifted, axis=1, keepdims=True))
    factor = lax.rsqrt(spread + EPSILON) * (1.0 / math.sqrt(length * channels))
    return (shifted * factor).astype(jnp.bfloat16)

def reference(series, tail, excl):
    count = S_DEV
    full = jnp.concatenate([series, tail], axis=1)
    total_len = series.shape[1]
    padded = jnp.concatenate([full, jnp.zeros((C, 2 * count), full.dtype)], axis=1)
    limit = excl[0]

    def one_block(block):
        start = block * count
        segment = lax.dynamic_slice_in_dim(padded, start, 3 * count + M - 1, 1)
        zed = normalize(segment, 3 * count, M, C)
        query = zed[:, :, :count].astype(jnp.float32)
        scores = jnp.einsum('cmp,cmq->pq', query, zed.astype(jnp.float32), precision=lax.Precision.HIGHEST)
        rows = start + jnp.arange(count, dtype=jnp.int32)[:, None]
        columns = start + jnp.arange(3 * count, dtype=jnp.int32)[None, :]
        keep = (jnp.abs(rows - columns) >= limit) & (columns < total_len)
        scored = jnp.where(keep, 1.0 - scores, CEILING)
        return (lax.optimization_barrier(jnp.min(scored, axis=1)), lax.optimization_barrier(jnp.min(scored[:, count:2 * count], axis=0)), lax.optimization_barrier(jnp.min(scored[:, 2 * count:], axis=0)))
    row_best, near_cols, far_cols = lax.map(one_block, jnp.arange(N_TM, dtype=jnp.int32))
    filler = jnp.full((2, count), CEILING, row_best.dtype)
    near_cols = jnp.concatenate([filler[:1], near_cols[:-1]], axis=0)
    far_cols = jnp.concatenate([filler, far_cols[:-2]], axis=0)
    return jnp.minimum(row_best, jnp.minimum(near_cols, far_cols)).reshape(-1)
```

```python
import math

import jax
import jax.numpy as jnp
from jax import lax
from jax.experimental import pallas as pl
from jax.experimental.pallas import tpu as pltpu
from jax.sharding import PartitionSpec as P

C = 64
M = 128
EPSILON = 1e-05
MASKED = -3.0

BLOCK = 512
HALO = 128
SPAN = BLOCK + HALO
GROUP = 32
COPIES = 4
ROWS = BLOCK + GROUP
MESH = pl.DeviceIdType.MESH
NT = (((1,), (1,)), ((), ()))


def spread_lanes(x):
    parts = [x[:, :ROWS]]
    for a in range(1, COPIES):
        parts.append(pltpu.roll(x, SPAN - GROUP * a, 1)[:, :ROWS])
    return jnp.concatenate(parts, axis=0).T


def statistics(y):
    total, moment, width = y, None, 1
    while width < GROUP:
        left, right = total[:-width], total[width:]
        delta = left - right
        delta = delta * delta * (0.5 / width)
        moment = delta if moment is None else moment[:-width] + moment[width:] + delta
        total = left + right
        width *= 2
    total, moment = total[:BLOCK], moment[:BLOCK]
    while width < M:
        other = pltpu.roll(total, width, 1)
        delta = total - other
        moment = moment + pltpu.roll(moment, width, 1) + delta * delta * (0.5 / width)
        total = total + other
        width *= 2
    center = total * (1.0 / M)
    factor = lax.rsqrt(moment * (1.0 / M) + EPSILON) * (1.0 / math.sqrt(M * C))
    return center, factor


def dot(left, right):
    return lax.dot_general(left, right, NT, preferred_element_type=jnp.float32)


def kernel(
    blocks, series, tail, excl, out,
    own, ahead, head, lanes, center, factor, zed,
    row_out, row_in, col_out, near_in, far_in,
    send, recv,
):
    t = lax.axis_index("tm")
    h = lax.axis_index("chan")

    def at(offset):
        return lax.rem(t + (offset + blocks), blocks)

    barrier = pltpu.get_barrier_semaphore()
    pl.semaphore_signal(barrier, inc=1, device_id=(t, 1 - h), device_id_type=MESH)
    for offset in (1, 2, 3):
        for chan in (0, 1):
            pl.semaphore_signal(
                barrier, inc=1, device_id=(at(offset), chan), device_id_type=MESH
            )
    own[0, :, :BLOCK] = series[...]
    head[...] = jnp.where(
        t == 0, jnp.concatenate([tail[...], jnp.zeros((GROUP, 1), jnp.float32)], axis=1),
        series[:, :HALO],
    )
    pl.semaphore_wait(barrier, 7)

    copies = []

    def push(source, target, index, device):
        copies.append(
            pltpu.make_async_remote_copy(
                src_ref=source,
                dst_ref=target,
                send_sem=send.at[len(copies)],
                recv_sem=recv.at[index],
                device_id=device,
                device_id_type=MESH,
            )
        )
        copies[-1].start()

    slot = (h, 1 - h)
    for chan in (0, 1):
        push(head, own.at[slot[chan], :, BLOCK:], 1 + slot[chan], (at(-1), chan))
    push(series, own.at[1, :, :BLOCK], 0, (t, 1 - h))
    for chan in (0, 1):
        push(series, ahead.at[slot[chan], :, :BLOCK], 3 + slot[chan], (at(-1 - chan), chan))
    for chan in (0, 1):
        push(head, ahead.at[slot[chan], :, BLOCK:], 5 + slot[chan], (at(-2 - chan), chan))

    def arrive(target, index):
        pltpu.make_async_remote_copy(
            src_ref=target,
            dst_ref=target,
            send_sem=send.at[0],
            recv_sem=recv.at[index],
            device_id=(t, 1 - h),
            device_id_type=MESH,
        ).wait_recv()

    def prepare(x, index):
        y = spread_lanes(x)
        lanes[index] = y
        mean, scale = statistics(y)
        center[index] = mean
        factor[index] = scale

    def normalized(index, step):
        parts = []
        for i in (2 * step, 2 * step + 1):
            shifted = lanes[index, i : i + BLOCK, :] - center[index]
            parts.append((shifted * factor[index]).astype(jnp.bfloat16))
        return parts

    half = BLOCK // 2
    same = None
    for s in (0, 1):
        if s == 1:
            arrive(own.at[1, :, :BLOCK], 0)
        arrive(own.at[s, :, BLOCK:], 1 + s)
        prepare(own[s], s)
        for step in range(GROUP // 2):
            parts = normalized(s, step)
            for j in (0, 1):
                zed[GROUP * s + 2 * step + j] = parts[j]
            query = jnp.concatenate(parts, axis=1)
            chosen = jnp.where(h == 0, query[:half], query[half:])
            product = dot(query, chosen)
            same = product if same is None else same + product

    cross = None
    for s in (0, 1):
        arrive(ahead.at[s, :, :BLOCK], 3 + s)
        arrive(ahead.at[s, :, BLOCK:], 5 + s)
        prepare(ahead[s], 2 + s)
        for step in range(GROUP // 2):
            k = GROUP * s + 2 * step
            query = jnp.concatenate([zed[k], zed[k + 1]], axis=1)
            product = dot(query, jnp.concatenate(normalized(2 + s, step), axis=1))
            cross = product if cross is None else cross + product

    limit = excl[0]
    apart = (
        lax.broadcasted_iota(jnp.int32, (BLOCK, half), 0)
        - lax.broadcasted_iota(jnp.int32, (BLOCK, half), 1)
        - half * h
    )
    same = jnp.where(jnp.abs(apart) >= limit, same, MASKED)

    reach = (
        lax.broadcasted_iota(jnp.int32, (HALO, HALO), 1)
        - lax.broadcasted_iota(jnp.int32, (HALO, HALO), 0)
        + (BLOCK * (1 + h) - (BLOCK - HALO))
    )
    corner = jnp.where(reach >= limit, cross[BLOCK - HALO :, :HALO], MASKED)
    first = jnp.concatenate([cross[: BLOCK - HALO, :HALO], corner], axis=0)
    tiles = [first] + [cross[:, HALO * j : HALO * (j + 1)] for j in range(1, BLOCK // HALO)]

    inside = t + 1 + h < blocks
    columns = jnp.concatenate([jnp.max(tile, axis=0, keepdims=True) for tile in tiles], axis=1)
    col_out[...] = jnp.where(inside, columns, MASKED)

    best = tiles[0]
    for tile in tiles[1:]:
        best = jnp.maximum(best, tile)
    best = jnp.where(inside, best, MASKED)
    best = jnp.maximum(best, jnp.maximum(same[:, :HALO], same[:, HALO:]))
    rows = jnp.max(best.T, axis=0, keepdims=True)
    row_out[...] = rows

    @pl.when(h == 0)
    def _():
        for chan in (0, 1):
            near = pltpu.make_async_remote_copy(
                src_ref=col_out, dst_ref=near_in, send_sem=send.at[7 + chan], recv_sem=recv.at[7],
                device_id=(at(1), chan), device_id_type=MESH,
            )
            near.start()

    @pl.when(h == 1)
    def _():
        for chan in (0, 1):
            far = pltpu.make_async_remote_copy(
                src_ref=col_out, dst_ref=far_in, send_sem=send.at[7 + chan], recv_sem=recv.at[8],
                device_id=(at(2), chan), device_id_type=MESH,
            )
            far.start()

    mine = pltpu.make_async_remote_copy(
        src_ref=row_out, dst_ref=row_in, send_sem=send.at[9], recv_sem=recv.at[9],
        device_id=(t, 1 - h), device_id_type=MESH,
    )
    mine.start()
    for copy in copies:
        copy.wait_send()
    arrive(near_in, 7)
    arrive(far_in, 8)
    mine.wait()
    for chan in (0, 1):
        pltpu.make_async_remote_copy(
            src_ref=col_out, dst_ref=near_in, send_sem=send.at[7 + chan], recv_sem=recv.at[7],
            device_id=(t, 1 - h), device_id_type=MESH,
        ).wait_send()
    best = jnp.maximum(jnp.maximum(row_out[...], row_in[...]), jnp.maximum(near_in[...], far_in[...]))
    out[...] = 1.0 - best


def solution(mesh):
    blocks = mesh.shape["tm"]

    def on_device(series, tail, excl):
        vmem = pl.BlockSpec(memory_space=pltpu.VMEM)
        f32 = jnp.float32
        result = pl.pallas_call(
            lambda *refs: kernel(blocks, *refs),
            out_shape=jax.ShapeDtypeStruct((1, BLOCK), f32),
            in_specs=[vmem, vmem, pl.BlockSpec(memory_space=pltpu.SMEM)],
            out_specs=vmem,
            scratch_shapes=[
                pltpu.VMEM((2, GROUP, SPAN), f32),
                pltpu.VMEM((2, GROUP, SPAN), f32),
                pltpu.VMEM((GROUP, HALO), f32),
                pltpu.VMEM((4, ROWS, M), f32),
                pltpu.VMEM((4, BLOCK, M), f32),
                pltpu.VMEM((4, BLOCK, M), f32),
                pltpu.VMEM((2 * GROUP, BLOCK, M), jnp.bfloat16),
            ]
            + [pltpu.VMEM((1, BLOCK), f32)] * 5
            + [pltpu.SemaphoreType.DMA((10,)), pltpu.SemaphoreType.DMA((10,))],
            compiler_params=pltpu.CompilerParams(
                collective_id=0, has_side_effects=True, vmem_limit_bytes=48 * 1024 * 1024
            ),
        )(series, tail, excl)
        return result.reshape(BLOCK)

    placed = (P("chan", "tm"), P("chan", None), P())
    return jax.shard_map(
        on_device, mesh=mesh, in_specs=placed, out_specs=P("tm"), check_vma=False
    )
```

```python
import math

import jax
import jax.numpy as jnp
from jax import lax
from jax.experimental import pallas as pl
from jax.experimental.pallas import tpu as pltpu
from jax.sharding import PartitionSpec as P

C = 64
M = 128
EPSILON = 1e-05
MASKED = -3.0

BLOCK = 512
HALO = 128
SPAN = BLOCK + HALO
GROUP = 32
COPIES = 4
ROWS = BLOCK + GROUP
MESH = pl.DeviceIdType.MESH
NT = (((1,), (1,)), ((), ()))


def spread_lanes(x):
    parts = [x[:, :ROWS]]
    for a in range(1, COPIES):
        parts.append(pltpu.roll(x, SPAN - GROUP * a, 1)[:, :ROWS])
    return jnp.concatenate(parts, axis=0).T


def statistics(y):
    total, moment, width = y, None, 1
    while width < GROUP:
        left, right = total[:-width], total[width:]
        delta = left - right
        delta = delta * delta * (0.5 / width)
        moment = delta if moment is None else moment[:-width] + moment[width:] + delta
        total = left + right
        width *= 2
    total, moment = total[:BLOCK], moment[:BLOCK]
    while width < M:
        other = pltpu.roll(total, width, 1)
        delta = total - other
        moment = moment + pltpu.roll(moment, width, 1) + delta * delta * (0.5 / width)
        total = total + other
        width *= 2
    center = total * (1.0 / M)
    factor = lax.rsqrt(moment * (1.0 / M) + EPSILON) * (1.0 / math.sqrt(M * C))
    return center, factor


def dot(left, right):
    return lax.dot_general(left, right, NT, preferred_element_type=jnp.float32)


def kernel(
    blocks, series, tail, excl, out,
    own, behind, rest, ending, lanes, center, factor, zed,
    row_out, row_in, col_out, near_in, far_in,
    local, send, recv, ready,
):
    t = lax.axis_index("tm")
    h = lax.axis_index("chan")
    after = jnp.minimum(blocks - 1 - t, 2)
    last = t == blocks - 1
    inside = t >= 1 + h

    fetch = pltpu.make_async_copy(series, own.at[0, :, :BLOCK], local.at[0])
    fetch.start()
    barrier = pltpu.get_barrier_semaphore()

    def signal(semaphore, device):
        pl.semaphore_signal(semaphore, inc=1, device_id=device, device_id_type=MESH)

    signal(barrier, (t, 1 - h))

    @pl.when(t >= 1)
    def _():
        for chan in (0, 1):
            signal(barrier, (t - 1, chan))

    @pl.when((h == 1) & (t >= 2))
    def _():
        for chan in (0, 1):
            signal(barrier, (t - 2, chan))

    pl.semaphore_wait(barrier, 1 + after + jnp.minimum(after, 1))

    def push(source, target, outgoing, incoming, device):
        return pltpu.make_async_remote_copy(
            src_ref=source,
            dst_ref=target,
            send_sem=send.at[outgoing],
            recv_sem=recv.at[incoming],
            device_id=device,
            device_id_type=MESH,
        )

    def arrive(target, index):
        push(target, target, 0, index, (t, 1 - h)).wait_recv()

    slot = (h, 1 - h)
    opening = series.at[:, :HALO]
    share = push(series, own.at[1, :, :BLOCK], 0, 0, (t, 1 - h))
    next_block = push(series, behind.at[slot[0], :, :BLOCK], 1, 3 + slot[0], (t + 1, 0))
    next_edge = push(opening, behind.at[slot[1], :, BLOCK:], 2, 5 + slot[1], (t + 1, 1))
    second_block = push(series, behind.at[slot[1], :, :BLOCK], 3, 3 + slot[1], (t + 2, 1))
    edges = [
        push(opening, own.at[slot[c], :, BLOCK:], 4 + c, 1 + slot[c], (t - 1, c)) for c in (0, 1)
    ]
    closing = push(ending, own.at[1, :, BLOCK:], 9, 2, (t, 1 - h))

    @pl.when(after >= 1)
    def _():
        for chan in (0, 1):
            signal(ready, (t + 1, chan))

    share.start()

    @pl.when(after >= 1)
    def _():
        next_block.start()

    @pl.when((after >= 1) & (t >= 1))
    def _():
        next_edge.start()

    @pl.when(after >= 2)
    def _():
        second_block.start()

    @pl.when(t >= 1)
    def _():
        pl.semaphore_wait(ready, 2)
        for edge in edges:
            edge.start()

    fetch.wait()

    @pl.when(last)
    def _():
        copy = pltpu.make_async_copy(tail, rest, local.at[1])
        copy.start()
        copy.wait()
        ending[...] = jnp.concatenate([rest[...], jnp.zeros((GROUP, 1), jnp.float32)], axis=1)
        own[0, :, BLOCK:] = ending[...]
        closing.start()

    @pl.when(jnp.logical_not(inside))
    def _():
        behind[...] = jnp.zeros_like(behind)

    def prepare(x, index):
        y = spread_lanes(x)
        lanes[index] = y
        mean, scale = statistics(y)
        center[index] = mean
        factor[index] = scale

    def normalized(index, step):
        parts = []
        for i in (2 * step, 2 * step + 1):
            shifted = lanes[index, i : i + BLOCK, :] - center[index]
            parts.append((shifted * factor[index]).astype(jnp.bfloat16))
        return parts

    half = BLOCK // 2
    same = None
    for s in (0, 1):
        if s == 1:
            arrive(own.at[1, :, :BLOCK], 0)
            arrive(own.at[1, :, BLOCK:], 2)
        else:

            @pl.when(jnp.logical_not(last))
            def _():
                arrive(own.at[0, :, BLOCK:], 1)

        prepare(own[s], s)
        for step in range(GROUP // 2):
            parts = normalized(s, step)
            for j in (0, 1):
                zed[GROUP * s + 2 * step + j] = parts[j]
            query = jnp.concatenate(parts, axis=1)
            chosen = jnp.where(h == 0, query[:half], query[half:])
            product = dot(query, chosen)
            same = product if same is None else same + product

    cross = None
    for s in (0, 1):

        @pl.when(inside)
        def _(s=s):
            arrive(behind.at[s, :, :BLOCK], 3 + s)

        @pl.when(inside & (h == 1))
        def _(s=s):
            arrive(behind.at[s, :, BLOCK:], 5 + s)

        edge = jnp.where(h == 0, own[s, :, :HALO], behind[s, :, BLOCK:])
        prepare(jnp.concatenate([behind[s, :, :BLOCK], edge], axis=1), 2 + s)
        for step in range(GROUP // 2):
            k = GROUP * s + 2 * step
            query = jnp.concatenate([zed[k], zed[k + 1]], axis=1)
            product = dot(query, jnp.concatenate(normalized(2 + s, step), axis=1))
            cross = product if cross is None else cross + product

    limit = excl[0]
    apart = (
        lax.broadcasted_iota(jnp.int32, (BLOCK, half), 0)
        - lax.broadcasted_iota(jnp.int32, (BLOCK, half), 1)
        - half * h
    )
    same = jnp.where(jnp.abs(apart) >= limit, same, MASKED)

    reach = (
        lax.broadcasted_iota(jnp.int32, (HALO, HALO), 0)
        - lax.broadcasted_iota(jnp.int32, (HALO, HALO), 1)
        + (HALO + BLOCK * h)
    )
    corner = jnp.where(reach >= limit, cross[:HALO, BLOCK - HALO :], MASKED)
    final = jnp.concatenate([corner, cross[HALO:, BLOCK - HALO :]], axis=0)
    tiles = [cross[:, HALO * j : HALO * (j + 1)] for j in range(BLOCK // HALO - 1)] + [final]

    columns = jnp.concatenate([jnp.max(tile, axis=0, keepdims=True) for tile in tiles], axis=1)
    col_out[...] = columns

    home = [push(col_out, near_in, 6 + c, 7, (t - 1, c)) for c in (0, 1)]
    home_far = [push(col_out, far_in, 6 + c, 8, (t - 2, c)) for c in (0, 1)]

    @pl.when(inside & (h == 0))
    def _():
        for copy in home:
            copy.start()

    @pl.when(inside & (h == 1))
    def _():
        for copy in home_far:
            copy.start()

    best = tiles[0]
    for tile in tiles[1:]:
        best = jnp.maximum(best, tile)
    best = jnp.where(inside, best, MASKED)
    best = jnp.maximum(best, jnp.maximum(same[:, :HALO], same[:, HALO:]))
    rows = jnp.max(best.T, axis=0, keepdims=True)
    row_out[...] = rows

    mine = push(row_out, row_in, 8, 9, (t, 1 - h))
    mine.start()
    share.wait_send()

    @pl.when(after >= 1)
    def _():
        next_block.wait_send()
        arrive(near_in, 7)

    @pl.when((after >= 1) & (t >= 1))
    def _():
        next_edge.wait_send()

    @pl.when(after >= 2)
    def _():
        second_block.wait_send()
        arrive(far_in, 8)

    @pl.when(after < 1)
    def _():
        near_in[...] = jnp.full_like(near_in, MASKED)
        closing.wait_send()

    @pl.when(after < 2)
    def _():
        far_in[...] = jnp.full_like(far_in, MASKED)

    @pl.when(t >= 1)
    def _():
        for edge in edges:
            edge.wait_send()

    @pl.when(inside)
    def _():
        for copy in home:
            copy.wait_send()

    mine.wait()
    best = jnp.maximum(jnp.maximum(row_out[...], row_in[...]), jnp.maximum(near_in[...], far_in[...]))
    out[...] = 1.0 - best


def solution(mesh):
    blocks = mesh.shape["tm"]

    def on_device(series, tail, excl):
        vmem = pl.BlockSpec(memory_space=pltpu.VMEM)
        hbm = pl.BlockSpec(memory_space=pl.ANY)
        f32 = jnp.float32
        result = pl.pallas_call(
            lambda *refs: kernel(blocks, *refs),
            out_shape=jax.ShapeDtypeStruct((1, BLOCK), f32),
            in_specs=[hbm, hbm, pl.BlockSpec(memory_space=pltpu.SMEM)],
            out_specs=vmem,
            scratch_shapes=[
                pltpu.VMEM((2, GROUP, SPAN), f32),
                pltpu.VMEM((2, GROUP, SPAN), f32),
                pltpu.VMEM((GROUP, M - 1), f32),
                pltpu.VMEM((GROUP, HALO), f32),
                pltpu.VMEM((4, ROWS, M), f32),
                pltpu.VMEM((4, BLOCK, M), f32),
                pltpu.VMEM((4, BLOCK, M), f32),
                pltpu.VMEM((2 * GROUP, BLOCK, M), jnp.bfloat16),
            ]
            + [pltpu.VMEM((1, BLOCK), f32)] * 5
            + [
                pltpu.SemaphoreType.DMA((2,)),
                pltpu.SemaphoreType.DMA((10,)),
                pltpu.SemaphoreType.DMA((10,)),
                pltpu.SemaphoreType.REGULAR,
            ],
            compiler_params=pltpu.CompilerParams(
                collective_id=0, has_side_effects=True, vmem_limit_bytes=64 * 1024 * 1024
            ),
        )(series, tail, excl)
        return result.reshape(BLOCK)

    placed = (P("chan", "tm"), P("chan", None), P())
    return jax.shard_map(
        on_device, mesh=mesh, in_specs=placed, out_specs=P("tm"), check_vma=False
    )
```

```python
import math

import jax
import jax.numpy as jnp
from jax import lax
from jax.experimental import pallas as pl
from jax.experimental.pallas import tpu as pltpu
from jax.sharding import PartitionSpec as P

C = 64
M = 128
EPSILON = 1e-05
MASKED = -3.0

BLOCK = 512
HALO = 128
SPAN = BLOCK + HALO
GROUP = 32
COPIES = 4
ROWS = BLOCK + GROUP
ROW = 16
MESH = pl.DeviceIdType.MESH
NT = (((1,), (1,)), ((), ()))


def spread_lanes(x):
    parts = [x[:, :ROWS]]
    for a in range(1, COPIES):
        parts.append(pltpu.roll(x, SPAN - GROUP * a, 1)[:, :ROWS])
    return jnp.concatenate(parts, axis=0).T


def statistics(y):
    total, moment, width = y, None, 1
    while width < GROUP:
        left, right = total[:-width], total[width:]
        delta = left - right
        delta = delta * delta * (0.5 / width)
        moment = delta if moment is None else moment[:-width] + moment[width:] + delta
        total = left + right
        width *= 2
    total, moment = total[:BLOCK], moment[:BLOCK]
    while width < M:
        other = pltpu.roll(total, width, 1)
        delta = total - other
        moment = moment + pltpu.roll(moment, width, 1) + delta * delta * (0.5 / width)
        total = total + other
        width *= 2
    center = total * (1.0 / M)
    factor = lax.rsqrt(moment * (1.0 / M) + EPSILON) * (1.0 / math.sqrt(M * C))
    return center, factor


def dot(left, right):
    return lax.dot_general(left, right, NT, preferred_element_type=jnp.float32)


def accumulate(totals, products):
    if totals is None:
        return products
    return [total + product for total, product in zip(totals, products)]


def kernel(
    blocks, series, tail, excl, out,
    own, behind, rest, ending, lanes, center, factor, zed,
    row_out, row_in, col_out, near_in, far_in,
    local, send, recv, ready,
):
    t = lax.axis_index("tm")
    h = lax.axis_index("chan")
    after = jnp.minimum(blocks - 1 - t, 2)
    last = t == blocks - 1
    inside = t >= 1 + h

    fetch = pltpu.make_async_copy(series, own.at[0, :, :BLOCK], local.at[0])
    fetch.start()
    barrier = pltpu.get_barrier_semaphore()

    def signal(semaphore, device):
        pl.semaphore_signal(semaphore, inc=1, device_id=device, device_id_type=MESH)

    opens_row = lax.rem(t, ROW) == 0
    closes_row = lax.rem(t, ROW) == ROW - 1
    signal(barrier, (t, 1 - h))

    @pl.when((after >= 1) & jnp.logical_not(closes_row))
    def _():
        for chan in (0, 1):
            signal(barrier, (t + 1, chan))

    @pl.when(t >= 1)
    def _():
        for chan in (0, 1):
            signal(barrier, (t - 1, chan))

    @pl.when((h == 1) & (t >= 2))
    def _():
        for chan in (0, 1):
            signal(barrier, (t - 2, chan))

    pl.semaphore_wait(barrier, 1 + after + jnp.minimum(after, 1) + 2 * jnp.minimum(lax.rem(t, ROW), 1))

    def push(source, target, outgoing, incoming, device):
        return pltpu.make_async_remote_copy(
            src_ref=source,
            dst_ref=target,
            send_sem=send.at[outgoing],
            recv_sem=recv.at[incoming],
            device_id=device,
            device_id_type=MESH,
        )

    def arrive(target, index):
        push(target, target, 0, index, (t, 1 - h)).wait_recv()

    slot = (h, 1 - h)
    opening = series.at[:, :HALO]
    share = push(series, own.at[1, :, :BLOCK], 0, 0, (t, 1 - h))
    next_block = push(series, behind.at[slot[0], :, :BLOCK], 1, 3 + slot[0], (t + 1, 0))
    next_edge = push(opening, behind.at[slot[1], :, BLOCK:], 2, 5 + slot[1], (t + 1, 1))
    second_block = push(series, behind.at[slot[1], :, :BLOCK], 3, 3 + slot[1], (t + 2, 1))
    edges = [
        push(opening, own.at[slot[c], :, BLOCK:], 4 + c, 1 + slot[c], (t - 1, c)) for c in (0, 1)
    ]
    closing = push(ending, own.at[1, :, BLOCK:], 9, 2, (t, 1 - h))

    @pl.when((after >= 1) & closes_row)
    def _():
        for chan in (0, 1):
            signal(ready, (t + 1, chan))

    @pl.when(jnp.logical_not(opens_row))
    def _():
        for edge in edges:
            edge.start()

    share.start()

    @pl.when(after >= 1)
    def _():
        next_block.start()

    @pl.when((after >= 1) & (t >= 1))
    def _():
        next_edge.start()

    @pl.when(after >= 2)
    def _():
        second_block.start()

    @pl.when(opens_row & (t >= 1))
    def _():
        pl.semaphore_wait(ready, 2)
        for edge in edges:
            edge.start()

    fetch.wait()

    @pl.when(last)
    def _():
        copy = pltpu.make_async_copy(tail, rest, local.at[1])
        copy.start()
        copy.wait()
        ending[...] = jnp.concatenate([rest[...], jnp.zeros((GROUP, 1), jnp.float32)], axis=1)
        own[0, :, BLOCK:] = ending[...]
        closing.start()

    @pl.when(jnp.logical_not(inside))
    def _():
        behind[...] = jnp.zeros_like(behind)

    def prepare(x, index):
        y = spread_lanes(x)
        lanes[index] = y
        mean, scale = statistics(y)
        center[index] = mean
        factor[index] = scale

    def normalized(index, step):
        parts = []
        for i in (2 * step, 2 * step + 1):
            shifted = lanes[index, i : i + BLOCK, :] - center[index]
            parts.append((shifted * factor[index]).astype(jnp.bfloat16))
        return parts

    half = BLOCK // 2
    same = None

    @pl.when(jnp.logical_not(last))
    def _():
        arrive(own.at[0, :, BLOCK:], 1)

    arrive(own.at[1, :, BLOCK:], 2)
    arrive(own.at[1, :, :BLOCK], 0)
    for s in (0, 1):
        prepare(own[s], s)
        for step in range(GROUP // 2):
            parts = normalized(s, step)
            for j in (0, 1):
                zed[GROUP * s + 2 * step + j] = parts[j]
            query = jnp.concatenate(parts, axis=1)
            chosen = jnp.where(h == 0, query[:half], query[half:])
            same = accumulate(same, [dot(query[:half], chosen), dot(query[half:], chosen)])

    @pl.when(inside)
    def _():
        for s in (0, 1):
            arrive(behind.at[s, :, :BLOCK], 3 + s)

    @pl.when(inside & (h == 1))
    def _():
        for s in (0, 1):
            arrive(behind.at[s, :, BLOCK:], 5 + s)

    cross = None
    for s in (0, 1):
        edge = jnp.where(h == 0, own[s, :, :HALO], behind[s, :, BLOCK:])
        prepare(jnp.concatenate([behind[s, :, :BLOCK], edge], axis=1), 2 + s)
        for step in range(GROUP // 2):
            k = GROUP * s + 2 * step
            query = jnp.concatenate([zed[k], zed[k + 1]], axis=1)
            key = jnp.concatenate(normalized(2 + s, step), axis=1)
            cross = accumulate(cross, [dot(query, key[:half]), dot(query, key[half:])])

    same = jnp.concatenate(same, axis=0)
    cross = jnp.concatenate(cross, axis=1)
    limit = excl[0]
    apart = (
        lax.broadcasted_iota(jnp.int32, (BLOCK, half), 0)
        - lax.broadcasted_iota(jnp.int32, (BLOCK, half), 1)
        - half * h
    )
    same = jnp.where(jnp.abs(apart) >= limit, same, MASKED)

    reach = (
        lax.broadcasted_iota(jnp.int32, (HALO, HALO), 0)
        - lax.broadcasted_iota(jnp.int32, (HALO, HALO), 1)
        + (HALO + BLOCK * h)
    )
    corner = jnp.where(reach >= limit, cross[:HALO, BLOCK - HALO :], MASKED)
    final = jnp.concatenate([corner, cross[HALO:, BLOCK - HALO :]], axis=0)
    tiles = [cross[:, HALO * j : HALO * (j + 1)] for j in range(BLOCK // HALO - 1)] + [final]

    columns = jnp.concatenate([jnp.max(tile, axis=0, keepdims=True) for tile in tiles], axis=1)
    col_out[...] = columns

    home = [push(col_out, near_in, 6 + c, 7, (t - 1, c)) for c in (0, 1)]
    home_far = [push(col_out, far_in, 6 + c, 8, (t - 2, c)) for c in (0, 1)]

    @pl.when(inside & (h == 0))
    def _():
        for copy in home:
            copy.start()

    @pl.when(inside & (h == 1))
    def _():
        for copy in home_far:
            copy.start()

    best = tiles[0]
    for tile in tiles[1:]:
        best = jnp.maximum(best, tile)
    best = jnp.where(inside, best, MASKED)
    best = jnp.maximum(best, jnp.maximum(same[:, :HALO], same[:, HALO:]))
    rows = jnp.max(best.T, axis=0, keepdims=True)
    row_out[...] = rows

    mine = push(row_out, row_in, 8, 9, (t, 1 - h))
    mine.start()
    share.wait_send()

    @pl.when(after >= 1)
    def _():
        next_block.wait_send()
        arrive(near_in, 7)

    @pl.when((after >= 1) & (t >= 1))
    def _():
        next_edge.wait_send()

    @pl.when(after >= 2)
    def _():
        second_block.wait_send()
        arrive(far_in, 8)

    @pl.when(after < 1)
    def _():
        near_in[...] = jnp.full_like(near_in, MASKED)
        closing.wait_send()

    @pl.when(after < 2)
    def _():
        far_in[...] = jnp.full_like(far_in, MASKED)

    @pl.when(t >= 1)
    def _():
        for edge in edges:
            edge.wait_send()

    @pl.when(inside)
    def _():
        for copy in home:
            copy.wait_send()

    mine.wait()
    best = jnp.maximum(jnp.maximum(row_out[...], row_in[...]), jnp.maximum(near_in[...], far_in[...]))
    out[...] = 1.0 - best


def solution(mesh):
    blocks = mesh.shape["tm"]

    def on_device(series, tail, excl):
        vmem = pl.BlockSpec(memory_space=pltpu.VMEM)
        hbm = pl.BlockSpec(memory_space=pl.ANY)
        f32 = jnp.float32
        result = pl.pallas_call(
            lambda *refs: kernel(blocks, *refs),
            out_shape=jax.ShapeDtypeStruct((1, BLOCK), f32),
            in_specs=[hbm, hbm, pl.BlockSpec(memory_space=pltpu.SMEM)],
            out_specs=vmem,
            scratch_shapes=[
                pltpu.VMEM((2, GROUP, SPAN), f32),
                pltpu.VMEM((2, GROUP, SPAN), f32),
                pltpu.VMEM((GROUP, M - 1), f32),
                pltpu.VMEM((GROUP, HALO), f32),
                pltpu.VMEM((4, ROWS, M), f32),
                pltpu.VMEM((4, BLOCK, M), f32),
                pltpu.VMEM((4, BLOCK, M), f32),
                pltpu.VMEM((2 * GROUP, BLOCK, M), jnp.bfloat16),
            ]
            + [pltpu.VMEM((1, BLOCK), f32)] * 5
            + [
                pltpu.SemaphoreType.DMA((2,)),
                pltpu.SemaphoreType.DMA((10,)),
                pltpu.SemaphoreType.DMA((10,)),
                pltpu.SemaphoreType.REGULAR,
            ],
            compiler_params=pltpu.CompilerParams(
                collective_id=0, has_side_effects=True, vmem_limit_bytes=64 * 1024 * 1024
            ),
        )(series, tail, excl)
        return result.reshape(BLOCK)

    placed = (P("chan", "tm"), P("chan", None), P())
    return jax.shard_map(
        on_device, mesh=mesh, in_specs=placed, out_specs=P("tm"), check_vma=False
    )
```

```python
import math

import jax
import jax.numpy as jnp
from jax import lax
from jax.experimental import pallas as pl
from jax.experimental.pallas import tpu as pltpu
from jax.sharding import PartitionSpec as P

C = 64
M = 128
EPSILON = 1e-05
MASKED = -3.0

BLOCK = 512
HALO = 128
SPAN = BLOCK + HALO
GROUP = 32
COPIES = 4
ROWS = BLOCK + GROUP
ROW = 16
MESH = pl.DeviceIdType.MESH
NT = (((1,), (1,)), ((), ()))


def spread_lanes(x):
    parts = [x[:, :ROWS]]
    for a in range(1, COPIES):
        parts.append(pltpu.roll(x, SPAN - GROUP * a, 1)[:, :ROWS])
    return jnp.concatenate(parts, axis=0).T


def statistics(y):
    total, moment, width = y, None, 1
    while width < GROUP:
        left, right = total[:-width], total[width:]
        delta = left - right
        delta = delta * delta * (0.5 / width)
        moment = delta if moment is None else moment[:-width] + moment[width:] + delta
        total = left + right
        width *= 2
    total, moment = total[:BLOCK], moment[:BLOCK]
    while width < M:
        other = pltpu.roll(total, width, 1)
        delta = total - other
        moment = moment + pltpu.roll(moment, width, 1) + delta * delta * (0.5 / width)
        total = total + other
        width *= 2
    center = total * (1.0 / M)
    factor = lax.rsqrt(moment * (1.0 / M) + EPSILON) * (1.0 / math.sqrt(M * C))
    return center, factor


def dot(left, right):
    return lax.dot_general(left, right, NT, preferred_element_type=jnp.float32)


def accumulate(totals, products):
    if totals is None:
        return products
    return [total + product for total, product in zip(totals, products)]


def kernel(
    blocks, series, tail, excl, out,
    own, behind, rest, ending, lanes, center, factor, zed, within,
    row_out, row_in, col_out, near_in, far_in,
    local, send, recv, ready,
):
    t = lax.axis_index("tm")
    h = lax.axis_index("chan")
    after = jnp.minimum(blocks - 1 - t, 2)
    last = t == blocks - 1
    inside = t >= 1 + h

    fetch = pltpu.make_async_copy(series, own.at[0, :, :BLOCK], local.at[0])
    fetch.start()
    barrier = pltpu.get_barrier_semaphore()

    def signal(semaphore, device):
        pl.semaphore_signal(semaphore, inc=1, device_id=device, device_id_type=MESH)

    opens_row = lax.rem(t, ROW) == 0
    closes_row = lax.rem(t, ROW) == ROW - 1
    ends_row = lax.rem(t, ROW) >= ROW - 2
    signal(barrier, (t, 1 - h))

    @pl.when((after >= 1) & jnp.logical_not(closes_row))
    def _():
        for chan in (0, 1):
            signal(barrier, (t + 1, chan))

    @pl.when(t >= 1)
    def _():
        for chan in (0, 1):
            signal(barrier, (t - 1, chan))

    @pl.when((h == 1) & (t >= 2))
    def _():
        for chan in (0, 1):
            signal(barrier, (t - 2, chan))

    pl.semaphore_wait(barrier, 1 + after + jnp.minimum(after, 1) + 2 * jnp.minimum(lax.rem(t, ROW), 1))

    def push(source, target, outgoing, incoming, device):
        return pltpu.make_async_remote_copy(
            src_ref=source,
            dst_ref=target,
            send_sem=send.at[outgoing],
            recv_sem=recv.at[incoming],
            device_id=device,
            device_id_type=MESH,
        )

    def arrive(target, index):
        push(target, target, 0, index, (t, 1 - h)).wait_recv()

    slot = (h, 1 - h)
    opening = series.at[:, :HALO]
    share = push(series, own.at[1, :, :BLOCK], 0, 0, (t, 1 - h))
    next_block = push(series, behind.at[slot[0], :, :BLOCK], 1, 3 + slot[0], (t + 1, 0))
    next_edge = push(opening, behind.at[slot[1], :, BLOCK:], 2, 5 + slot[1], (t + 1, 1))
    second_block = push(series, behind.at[slot[1], :, :BLOCK], 3, 3 + slot[1], (t + 2, 1))
    edges = [
        push(opening, own.at[slot[c], :, BLOCK:], 4 + c, 1 + slot[c], (t - 1, c)) for c in (0, 1)
    ]
    closing = push(ending, own.at[1, :, BLOCK:], 9, 2, (t, 1 - h))

    @pl.when((after >= 1) & closes_row)
    def _():
        for chan in (0, 1):
            signal(ready, (t + 1, chan))

    def send_ahead():
        @pl.when(after >= 1)
        def _():
            next_block.start()

        @pl.when((after >= 1) & (t >= 1))
        def _():
            next_edge.start()

        @pl.when(after >= 2)
        def _():
            second_block.start()

    pl.when(ends_row)(send_ahead)

    @pl.when(jnp.logical_not(opens_row))
    def _():
        for edge in edges:
            edge.start()

    share.start()
    pl.when(jnp.logical_not(ends_row))(send_ahead)

    @pl.when(opens_row & (t >= 1))
    def _():
        pl.semaphore_wait(ready, 2)
        for edge in edges:
            edge.start()

    fetch.wait()

    @pl.when(last)
    def _():
        copy = pltpu.make_async_copy(tail, rest, local.at[1])
        copy.start()
        copy.wait()
        ending[...] = jnp.concatenate([rest[...], jnp.zeros((GROUP, 1), jnp.float32)], axis=1)
        own[0, :, BLOCK:] = ending[...]
        closing.start()

    @pl.when(jnp.logical_not(inside))
    def _():
        behind[...] = jnp.zeros_like(behind)

    def prepare(x, index):
        y = spread_lanes(x)
        lanes[index] = y
        mean, scale = statistics(y)
        center[index] = mean
        factor[index] = scale

    def normalized(index, step):
        parts = []
        for i in (2 * step, 2 * step + 1):
            shifted = lanes[index, i : i + BLOCK, :] - center[index]
            parts.append((shifted * factor[index]).astype(jnp.bfloat16))
        return parts

    def receive(s):
        @pl.when(inside)
        def _():
            arrive(behind.at[s, :, :BLOCK], 3 + s)

        @pl.when(inside & (h == 1))
        def _():
            arrive(behind.at[s, :, BLOCK:], 5 + s)

    def prepare_behind(s):
        edge = jnp.where(h == 0, own[s, :, :HALO], behind[s, :, BLOCK:])
        prepare(jnp.concatenate([behind[s, :, :BLOCK], edge], axis=1), 2 + s)

    @pl.when(closes_row)
    def _():
        receive(0)
        prepare_behind(0)

    half = BLOCK // 2
    same = None

    @pl.when(jnp.logical_not(last))
    def _():
        arrive(own.at[0, :, BLOCK:], 1)

    prepare(own[0], 0)
    arrive(own.at[1, :, BLOCK:], 2)
    arrive(own.at[1, :, :BLOCK], 0)
    for s in (0, 1):
        if s == 1:
            prepare(own[1], 1)
        for step in range(GROUP // 2):
            parts = normalized(s, step)
            for j in (0, 1):
                zed[GROUP * s + 2 * step + j] = parts[j]
            query = jnp.concatenate(parts, axis=1)
            chosen = jnp.where(h == 0, query[:half], query[half:])
            same = accumulate(same, [dot(query[:half], chosen), dot(query[half:], chosen)])

    limit = excl[0]
    same = jnp.concatenate(same, axis=0)
    apart = (
        lax.broadcasted_iota(jnp.int32, (BLOCK, half), 0)
        - lax.broadcasted_iota(jnp.int32, (BLOCK, half), 1)
        - half * h
    )
    same = jnp.where(jnp.abs(apart) >= limit, same, MASKED)
    within[...] = jnp.maximum(same[:, :HALO], same[:, HALO:])

    @pl.when(jnp.logical_not(closes_row))
    def _():
        receive(0)
        prepare_behind(0)

    receive(1)
    cross = None
    for s in (0, 1):
        if s == 1:
            prepare_behind(1)
        for step in range(GROUP // 2):
            k = GROUP * s + 2 * step
            query = jnp.concatenate([zed[k], zed[k + 1]], axis=1)
            key = jnp.concatenate(normalized(2 + s, step), axis=1)
            cross = accumulate(cross, [dot(query, key[:half]), dot(query, key[half:])])

    cross = jnp.concatenate(cross, axis=1)

    reach = (
        lax.broadcasted_iota(jnp.int32, (HALO, HALO), 0)
        - lax.broadcasted_iota(jnp.int32, (HALO, HALO), 1)
        + (HALO + BLOCK * h)
    )
    corner = jnp.where(reach >= limit, cross[:HALO, BLOCK - HALO :], MASKED)
    final = jnp.concatenate([corner, cross[HALO:, BLOCK - HALO :]], axis=0)
    tiles = [cross[:, HALO * j : HALO * (j + 1)] for j in range(BLOCK // HALO - 1)] + [final]

    columns = jnp.concatenate([jnp.max(tile, axis=0, keepdims=True) for tile in tiles], axis=1)
    col_out[...] = columns

    home = [push(col_out, near_in, 6 + c, 7, (t - 1, c)) for c in (0, 1)]
    home_far = [push(col_out, far_in, 6 + c, 8, (t - 2, c)) for c in (0, 1)]

    @pl.when(inside & (h == 0))
    def _():
        for copy in home:
            copy.start()

    @pl.when(inside & (h == 1))
    def _():
        for copy in home_far:
            copy.start()

    best = tiles[0]
    for tile in tiles[1:]:
        best = jnp.maximum(best, tile)
    best = jnp.where(inside, best, MASKED)
    best = jnp.maximum(best, within[...])
    rows = jnp.max(best.T, axis=0, keepdims=True)
    row_out[...] = rows

    mine = push(row_out, row_in, 8, 9, (t, 1 - h))
    mine.start()
    share.wait_send()

    @pl.when(after >= 1)
    def _():
        next_block.wait_send()
        arrive(near_in, 7)

    @pl.when((after >= 1) & (t >= 1))
    def _():
        next_edge.wait_send()

    @pl.when(after >= 2)
    def _():
        second_block.wait_send()
        arrive(far_in, 8)

    @pl.when(after < 1)
    def _():
        near_in[...] = jnp.full_like(near_in, MASKED)
        closing.wait_send()

    @pl.when(after < 2)
    def _():
        far_in[...] = jnp.full_like(far_in, MASKED)

    @pl.when(t >= 1)
    def _():
        for edge in edges:
            edge.wait_send()

    @pl.when(inside)
    def _():
        for copy in home:
            copy.wait_send()

    mine.wait()
    best = jnp.maximum(jnp.maximum(row_out[...], row_in[...]), jnp.maximum(near_in[...], far_in[...]))
    out[...] = 1.0 - best


def solution(mesh):
    blocks = mesh.shape["tm"]

    def on_device(series, tail, excl):
        vmem = pl.BlockSpec(memory_space=pltpu.VMEM)
        hbm = pl.BlockSpec(memory_space=pl.ANY)
        f32 = jnp.float32
        result = pl.pallas_call(
            lambda *refs: kernel(blocks, *refs),
            out_shape=pltpu.VMEM((1, BLOCK), f32),
            in_specs=[hbm, hbm, pl.BlockSpec(memory_space=pltpu.SMEM)],
            out_specs=vmem,
            scratch_shapes=[
                pltpu.VMEM((2, GROUP, SPAN), f32),
                pltpu.VMEM((2, GROUP, SPAN), f32),
                pltpu.VMEM((GROUP, M - 1), f32),
                pltpu.VMEM((GROUP, HALO), f32),
                pltpu.VMEM((4, ROWS, M), f32),
                pltpu.VMEM((4, BLOCK, M), f32),
                pltpu.VMEM((4, BLOCK, M), f32),
                pltpu.VMEM((2 * GROUP, BLOCK, M), jnp.bfloat16),
                pltpu.VMEM((BLOCK, HALO), f32),
            ]
            + [pltpu.VMEM((1, BLOCK), f32)] * 5
            + [
                pltpu.SemaphoreType.DMA((2,)),
                pltpu.SemaphoreType.DMA((10,)),
                pltpu.SemaphoreType.DMA((10,)),
                pltpu.SemaphoreType.REGULAR,
            ],
            compiler_params=pltpu.CompilerParams(
                collective_id=0, has_side_effects=True, vmem_limit_bytes=60 * 1024 * 1024
            ),
        )(series, tail, excl)
        return result.reshape(BLOCK)

    placed = (P("chan", "tm"), P("chan", None), P())
    return jax.shard_map(
        on_device, mesh=mesh, in_specs=placed, out_specs=P("tm"), check_vma=False
    )
```

```python
import math

import jax
import jax.numpy as jnp
from jax import lax
from jax.experimental import pallas as pl
from jax.experimental.pallas import tpu as pltpu
from jax.sharding import PartitionSpec as P

C = 64
M = 128
EPSILON = 1e-05
MASKED = -3.0

BLOCK = 512
HALO = 128
SPAN = BLOCK + HALO
GROUP = 32
COPIES = 4
ROWS = BLOCK + GROUP
ROW = 16
MESH = pl.DeviceIdType.MESH
NT = (((1,), (1,)), ((), ()))


def spread_lanes(x):
    parts = [x[:, :ROWS]]
    for a in range(1, COPIES):
        parts.append(pltpu.roll(x, SPAN - GROUP * a, 1)[:, :ROWS])
    return jnp.concatenate(parts, axis=0).T


def statistics(y):
    total, moment, width = y, None, 1
    while width < GROUP:
        left, right = total[:-width], total[width:]
        delta = left - right
        delta = delta * delta * (0.5 / width)
        moment = delta if moment is None else moment[:-width] + moment[width:] + delta
        total = left + right
        width *= 2
    total, moment = total[:BLOCK], moment[:BLOCK]
    while width < M:
        other = pltpu.roll(total, width, 1)
        delta = total - other
        moment = moment + pltpu.roll(moment, width, 1) + delta * delta * (0.5 / width)
        total = total + other
        width *= 2
    center = total * (1.0 / M)
    factor = lax.rsqrt(moment * (1.0 / M) + EPSILON) * (1.0 / math.sqrt(M * C))
    return center, factor


def dot(left, right):
    return lax.dot_general(left, right, NT, preferred_element_type=jnp.float32)


def accumulate(totals, products):
    if totals is None:
        return products
    return [total + product for total, product in zip(totals, products)]


def kernel(
    blocks, series, tail, excl, out,
    own, behind, rest, ending, lanes, center, factor, zed, within,
    row_out, row_in, col_out, near_in, far_in,
    local, send, recv, ready,
):
    t = lax.axis_index("tm")
    h = lax.axis_index("chan")
    after = jnp.minimum(blocks - 1 - t, 2)
    last = t == blocks - 1
    inside = t >= 1 + h

    fetch = pltpu.make_async_copy(series, own.at[0, :, :BLOCK], local.at[0])
    fetch.start()
    barrier = pltpu.get_barrier_semaphore()

    def signal(semaphore, device):
        pl.semaphore_signal(semaphore, inc=1, device_id=device, device_id_type=MESH)

    opens_row = lax.rem(t, ROW) == 0
    closes_row = lax.rem(t, ROW) == ROW - 1
    ends_row = lax.rem(t, ROW) >= ROW - 2
    signal(barrier, (t, 1 - h))

    @pl.when((after >= 1) & jnp.logical_not(closes_row))
    def _():
        for chan in (0, 1):
            signal(barrier, (t + 1, chan))

    @pl.when(t >= 1)
    def _():
        for chan in (0, 1):
            signal(barrier, (t - 1, chan))

    @pl.when((h == 1) & (t >= 2))
    def _():
        for chan in (0, 1):
            signal(barrier, (t - 2, chan))

    pl.semaphore_wait(barrier, 1 + after + jnp.minimum(after, 1) + 2 * jnp.minimum(lax.rem(t, ROW), 1))

    def push(source, target, outgoing, incoming, device):
        return pltpu.make_async_remote_copy(
            src_ref=source,
            dst_ref=target,
            send_sem=send.at[outgoing],
            recv_sem=recv.at[incoming],
            device_id=device,
            device_id_type=MESH,
        )

    def arrive(target, index):
        push(target, target, 0, index, (t, 1 - h)).wait_recv()

    slot = (h, 1 - h)
    opening = series.at[:, :HALO]
    share = push(series, own.at[1, :, :BLOCK], 0, 0, (t, 1 - h))
    next_block = push(series, behind.at[slot[0], :, :BLOCK], 1, 3 + slot[0], (t + 1, 0))
    next_edge = push(opening, behind.at[slot[1], :, BLOCK:], 2, 5 + slot[1], (t + 1, 1))
    second_block = push(series, behind.at[slot[1], :, :BLOCK], 3, 3 + slot[1], (t + 2, 1))
    edges = [
        push(opening, own.at[slot[c], :, BLOCK:], 4 + c, 1 + slot[c], (t - 1, c)) for c in (0, 1)
    ]
    closing = push(ending, own.at[1, :, BLOCK:], 9, 2, (t, 1 - h))

    @pl.when((after >= 1) & closes_row)
    def _():
        for chan in (0, 1):
            signal(ready, (t + 1, chan))

    def send_ahead():
        @pl.when(after >= 1)
        def _():
            next_block.start()

        @pl.when((after >= 1) & (t >= 1))
        def _():
            next_edge.start()

        @pl.when(after >= 2)
        def _():
            second_block.start()

    pl.when(ends_row)(send_ahead)

    @pl.when(jnp.logical_not(opens_row))
    def _():
        for edge in edges:
            edge.start()

    share.start()
    pl.when(jnp.logical_not(ends_row))(send_ahead)

    @pl.when(opens_row & (t >= 1))
    def _():
        pl.semaphore_wait(ready, 2)
        for edge in edges:
            edge.start()

    fetch.wait()

    @pl.when(last)
    def _():
        copy = pltpu.make_async_copy(tail, rest, local.at[1])
        copy.start()
        copy.wait()
        ending[...] = jnp.concatenate([rest[...], jnp.zeros((GROUP, 1), jnp.float32)], axis=1)
        own[0, :, BLOCK:] = ending[...]
        closing.start()

    @pl.when(jnp.logical_not(inside))
    def _():
        behind[...] = jnp.zeros_like(behind)

    def prepare(x, index):
        y = spread_lanes(x)
        lanes[index] = y
        mean, scale = statistics(y)
        center[index] = mean
        factor[index] = scale

    def normalized(index, step):
        parts = []
        for i in (2 * step, 2 * step + 1):
            shifted = lanes[index, i : i + BLOCK, :] - center[index]
            parts.append((shifted * factor[index]).astype(jnp.bfloat16))
        return parts

    def receive(s):
        @pl.when(inside)
        def _():
            arrive(behind.at[s, :, :BLOCK], 3 + s)

        @pl.when(inside & (h == 1))
        def _():
            arrive(behind.at[s, :, BLOCK:], 5 + s)

    def prepare_behind(s):
        edge = jnp.where(h == 0, own[s, :, :HALO], behind[s, :, BLOCK:])
        prepare(jnp.concatenate([behind[s, :, :BLOCK], edge], axis=1), 2 + s)

    @pl.when(closes_row)
    def _():
        receive(0)
        prepare_behind(0)

    half = BLOCK // 2
    same = None

    @pl.when(jnp.logical_not(last))
    def _():
        arrive(own.at[0, :, BLOCK:], 1)

    for s in (0, 1):
        if s == 1:
            arrive(own.at[1, :, BLOCK:], 2)
            arrive(own.at[1, :, :BLOCK], 0)
        prepare(own[s], s)
        for step in range(GROUP // 2):
            parts = normalized(s, step)
            for j in (0, 1):
                zed[GROUP * s + 2 * step + j] = parts[j]
            query = jnp.concatenate(parts, axis=1)
            chosen = jnp.where(h == 0, query[:half], query[half:])
            same = accumulate(same, [dot(query[:half], chosen), dot(query[half:], chosen)])

    limit = excl[0]
    same = jnp.concatenate(same, axis=0)
    apart = (
        lax.broadcasted_iota(jnp.int32, (BLOCK, half), 0)
        - lax.broadcasted_iota(jnp.int32, (BLOCK, half), 1)
        - half * h
    )
    same = jnp.where(jnp.abs(apart) >= limit, same, MASKED)
    within[...] = jnp.maximum(same[:, :HALO], same[:, HALO:])

    @pl.when(jnp.logical_not(closes_row))
    def _():
        receive(0)
        prepare_behind(0)

    receive(1)
    cross = None
    for s in (0, 1):
        if s == 1:
            prepare_behind(1)
        for step in range(GROUP // 2):
            k = GROUP * s + 2 * step
            query = jnp.concatenate([zed[k], zed[k + 1]], axis=1)
            key = jnp.concatenate(normalized(2 + s, step), axis=1)
            cross = accumulate(cross, [dot(query, key[:half]), dot(query, key[half:])])

    cross = jnp.concatenate(cross, axis=1)

    reach = (
        lax.broadcasted_iota(jnp.int32, (HALO, HALO), 0)
        - lax.broadcasted_iota(jnp.int32, (HALO, HALO), 1)
        + (HALO + BLOCK * h)
    )
    corner = jnp.where(reach >= limit, cross[:HALO, BLOCK - HALO :], MASKED)
    final = jnp.concatenate([corner, cross[HALO:, BLOCK - HALO :]], axis=0)
    tiles = [cross[:, HALO * j : HALO * (j + 1)] for j in range(BLOCK // HALO - 1)] + [final]

    columns = jnp.concatenate([jnp.max(tile, axis=0, keepdims=True) for tile in tiles], axis=1)
    col_out[...] = columns

    home = [push(col_out, near_in, 6 + c, 7, (t - 1, c)) for c in (0, 1)]
    home_far = [push(col_out, far_in, 6 + c, 8, (t - 2, c)) for c in (0, 1)]

    @pl.when(inside & (h == 0))
    def _():
        for copy in home:
            copy.start()

    @pl.when(inside & (h == 1))
    def _():
        for copy in home_far:
            copy.start()

    best = tiles[0]
    for tile in tiles[1:]:
        best = jnp.maximum(best, tile)
    best = jnp.where(inside, best, MASKED)
    best = jnp.maximum(best, within[...])
    rows = jnp.max(best.T, axis=0, keepdims=True)
    row_out[...] = rows

    mine = push(row_out, row_in, 8, 9, (t, 1 - h))
    mine.start()
    share.wait_send()

    @pl.when(after >= 1)
    def _():
        next_block.wait_send()
        arrive(near_in, 7)

    @pl.when((after >= 1) & (t >= 1))
    def _():
        next_edge.wait_send()

    @pl.when(after >= 2)
    def _():
        second_block.wait_send()
        arrive(far_in, 8)

    @pl.when(after < 1)
    def _():
        near_in[...] = jnp.full_like(near_in, MASKED)
        closing.wait_send()

    @pl.when(after < 2)
    def _():
        far_in[...] = jnp.full_like(far_in, MASKED)

    @pl.when(t >= 1)
    def _():
        for edge in edges:
            edge.wait_send()

    @pl.when(inside)
    def _():
        for copy in home:
            copy.wait_send()

    mine.wait()
    best = jnp.maximum(jnp.maximum(row_out[...], row_in[...]), jnp.maximum(near_in[...], far_in[...]))
    out[...] = 1.0 - best


def solution(mesh):
    blocks = mesh.shape["tm"]

    def on_device(series, tail, excl):
        vmem = pl.BlockSpec(memory_space=pltpu.VMEM)
        hbm = pl.BlockSpec(memory_space=pl.ANY)
        f32 = jnp.float32
        result = pl.pallas_call(
            lambda *refs: kernel(blocks, *refs),
            out_shape=pltpu.VMEM((1, BLOCK), f32),
            in_specs=[hbm, hbm, pl.BlockSpec(memory_space=pltpu.SMEM)],
            out_specs=vmem,
            scratch_shapes=[
                pltpu.VMEM((2, GROUP, SPAN), f32),
                pltpu.VMEM((2, GROUP, SPAN), f32),
                pltpu.VMEM((GROUP, M - 1), f32),
                pltpu.VMEM((GROUP, HALO), f32),
                pltpu.VMEM((4, ROWS, M), f32),
                pltpu.VMEM((4, BLOCK, M), f32),
                pltpu.VMEM((4, BLOCK, M), f32),
                pltpu.VMEM((2 * GROUP, BLOCK, M), jnp.bfloat16),
                pltpu.VMEM((BLOCK, HALO), f32),
            ]
            + [pltpu.VMEM((1, BLOCK), f32)] * 5
            + [
                pltpu.SemaphoreType.DMA((2,)),
                pltpu.SemaphoreType.DMA((10,)),
                pltpu.SemaphoreType.DMA((10,)),
                pltpu.SemaphoreType.REGULAR,
            ],
            compiler_params=pltpu.CompilerParams(
                collective_id=0, has_side_effects=True, vmem_limit_bytes=60 * 1024 * 1024
            ),
        )(series, tail, excl)
        return result.reshape(BLOCK)

    placed = (P("chan", "tm"), P("chan", None), P())
    return jax.shard_map(
        on_device, mesh=mesh, in_specs=placed, out_specs=P("tm"), check_vma=False
    )
```
